32 devices in a mesh: section: 4 (over y, x), shard: 8 (over z, core).
Axes of the slice: x: 2, y: 2, z: 4, core: 2. Of those that a mesh axis runs over, the one named last changes fastest.
Arguments:
- activations: bfloat16 [4, 768, 4096], P('section', 'shard'), may hold values from -30 to 30, as said below
- top_grad: bfloat16 [768, 4096], P('shard'), may hold values from -6 to 6
- loss_mask: int32 [768], P('shard'), may hold values 0 or 1
- norm_gain: float32 [4, 4096], P('section'), may hold values from 0.5 to 1.5
- value_weight: bfloat16 [4, 4096, 1024], P('section', 'shard'), may hold values from -0.046875 to 0.046875
- output_weight: bfloat16 [4, 1024, 4096], P('section', None, 'shard'), may hold values from -0.09375 to 0.09375
- value_proj: bfloat16 [4, 1024, 64], P('section'), may hold values from -0.1875 to 0.1875
- grad_proj: bfloat16 [4, 4096, 64], P('section'), may hold values from -0.09375 to 0.09375
- store: float32 [4, 1024, 4096], P('section', 'shard'), may hold values from -0.024 to 0.024
Outputs:
- scores: float32 [8, 1024], P('section', 'shard')
The draws below stay inside these ranges and needn't reach their ends.
Inputs may be any that keep to these rules, and one draw needn't show every extreme that they name: activations of order one per token.
All inputs are finite; a program needn't handle non-finite values. No bound on the sum of `loss_mask` on one device may be relied on, other than what follows from the above.
Results may differ from the reference program's by a relative error of at most 0.007.
Values may be sent and summed in bfloat16 or wider, within the bound.
No kernel may reach another device: no remote copies, remote signals or barrier semaphores. Data moves between devices by JAX's collectives and lax.ppermute only.
A program may use at most 128 MiB of HBM per device.

```python
import jax
import jax.numpy as jnp
from jax import lax

D = 4096
KV = 1024
PROJ = 64
LEN = 96
LAYERS = 4
GENS = 8
TOKENS = 768
STORE = 1024


def draw_activations(key, part):
    key_base, key_column, key_row = jax.random.split(key, 3)
    grid_shape = (LAYERS, TOKENS, D)
    sample_base = jnp.clip(jax.random.normal(key_base, grid_shape, jnp.float32), -5.0, 5.0)
    column_scale = jnp.exp(jax.random.uniform(key_column, (LAYERS, 1, D), jnp.float32, -1.1, 1.1))
    row_scale = jnp.exp(jax.random.uniform(key_row, (LAYERS, TOKENS, 1), jnp.float32, -0.69, 0.69))
    return (sample_base * column_scale * row_scale).astype(jnp.bfloat16)


def with_ends(values, own_key, smallest, largest):
    extent = values.shape
    spot = [jax.random.randint(jax.random.fold_in(own_key, axis), (), 0, extent[axis]) for axis in range(len(extent))]
    values = values.at[tuple(spot)].set(smallest)
    longest = extent.index(max(extent))
    spot[longest] = (spot[longest] + 1) % extent[longest]
    return values.at[tuple(spot)].set(largest)


def steps_of(stream_key, extent, cuts, smallest, high):
    def one(axis_at, shards_of):
        heights = jax.random.uniform(jax.random.fold_in(jax.random.fold_in(stream_key, 6), axis_at), (shards_of,), jnp.float32, smallest / len(cuts), high / len(cuts))
        return jnp.repeat(jnp.exp(heights), extent[axis_at] // shards_of).reshape((-1,) + (1,) * (len(extent) - axis_at - 1))

    factor_of = one(*cuts[0])
    for cut in cuts[1:]:
        factor_of = factor_of * one(*cut)
    return factor_of


def bell_draw(rng, shape, width, reach, pieces=(), held_as=jnp.bfloat16):
    result = width * jax.random.normal(rng, shape, jnp.float32)
    if pieces:
        result = result * steps_of(rng, shape, pieces, -0.22, 0.18)
    return jnp.clip(result, -reach, reach).astype(held_as)


def setup_inputs(seed: int = 0) -> dict:
    seeds = jax.random.split(jax.random.key(seed), 10)
    activations = draw_activations(jax.random.fold_in(seeds[9], 71), 0)
    top_grad = bell_draw(seeds[1], (TOKENS, D), 1.0, 6.0, ((0, 8),))
    loss_mask = with_ends((jax.random.randint(seeds[2], (TOKENS,), 0, 4) < 3).astype(jnp.int32), jax.random.fold_in(seeds[2], 1), 0, 1)
    norm_gain = jnp.clip(1.0 + 0.1 * jax.random.normal(seeds[3], (LAYERS, D), jnp.float32), 0.5, 1.5)
    value_weight = bell_draw(seeds[4], (LAYERS, D, KV), (4 * D) ** -0.5, 0.046875, ((0, 4), (1, 8)))
    output_weight = bell_draw(seeds[5], (LAYERS, KV, D), D ** -0.5, 0.09375, ((0, 4), (2, 8)))
    value_proj = bell_draw(seeds[6], (LAYERS, KV, PROJ), KV ** -0.5, 0.1875, ((0, 4),))
    grad_proj = bell_draw(seeds[7], (LAYERS, D, PROJ), D ** -0.5, 0.09375, ((0, 4),))
    store = bell_draw(seeds[8], (LAYERS, STORE, PROJ * PROJ), 0.004, 0.024, ((0, 4), (1, 8)), jnp.float32)
    return {"activations": activations, "top_grad": top_grad, "loss_mask": loss_mask, "norm_gain": norm_gain, "value_weight": value_weight, "output_weight": output_weight, "value_proj": value_proj, "grad_proj": grad_proj, "store": store}


EPSILON = 1e-05

def reference(activations, top_grad, loss_mask, norm_gain, value_weight, output_weight, value_proj, grad_proj, store):
    cotangent = (top_grad.astype(jnp.float32) * loss_mask.astype(jnp.float32)[:, None]).astype(jnp.bfloat16)
    score_total = jnp.zeros((GENS, STORE), jnp.float32)
    for layer_index in range(LAYERS - 1, -1, -1):
        hidden_in = activations[layer_index].astype(jnp.float32)
        inverse_rms = lax.rsqrt(lax.optimization_barrier(jnp.mean(hidden_in * hidden_in, axis=-1, keepdims=True)) + EPSILON)
        norm_scale = norm_gain[layer_index]
        normed = (hidden_in * inverse_rms * norm_scale).astype(jnp.bfloat16)
        value_act = jnp.dot(normed, value_weight[layer_index], preferred_element_type=jnp.float32).astype(jnp.bfloat16)
        value_low = jnp.dot(value_act, value_proj[layer_index], preferred_element_type=jnp.float32)
        grad_low = jnp.dot(cotangent, grad_proj[layer_index], preferred_element_type=jnp.float32)
        features = jnp.einsum('gta,gtb->gab', grad_low.reshape(GENS, LEN, PROJ), value_low.reshape(GENS, LEN, PROJ), precision=lax.Precision.HIGHEST).reshape(GENS, PROJ * PROJ)
        score_total = score_total + lax.dot_general(features, store[layer_index], (((1,), (1,)), ((), ())), precision=lax.Precision.HIGHEST, preferred_element_type=jnp.float32)
        if layer_index > 0:
            grad_value = lax.dot_general(cotangent, output_weight[layer_index], (((1,), (1,)), ((), ())), preferred_element_type=jnp.float32).astype(jnp.bfloat16)
            grad_normed = lax.dot_general(grad_value, value_weight[layer_index], (((1,), (1,)), ((), ())), preferred_element_type=jnp.float32)
            scaled = norm_scale * grad_normed
            correction = lax.optimization_barrier(jnp.mean(scaled * hidden_in, axis=-1, keepdims=True))
            grad_input = inverse_rms * scaled - hidden_in * (inverse_rms * inverse_rms * inverse_rms) * correction
            cotangent = (cotangent.astype(jnp.float32) + grad_input).astype(jnp.bfloat16)
    return score_total
```

```python
import jax
import jax.numpy as jnp
from jax import lax
from jax.sharding import PartitionSpec as P

LEN = 96
EPSILON = 1e-05
BF16 = jnp.bfloat16
F32 = jnp.float32


def swap(value, axis, step):
    return lax.ppermute(value, axis, [(i, i ^ step) for i in range(lax.axis_size(axis))])


def spread(rows):
    count = lax.axis_size("shard")
    index = lax.axis_index("shard")
    half = count // 2
    width = rows.shape[1] // count

    def piece(step):
        return lax.dynamic_slice_in_dim(rows, (index ^ step) * width, width, 1)

    keep = jnp.stack([piece(2 * z) for z in range(half)])
    away = jnp.stack([piece(2 * z + 1) for z in range(half)])
    both = [keep, swap(away, "shard", 1)]
    got = [jnp.stack([part[0] for part in both])]
    for z in range(1, half):
        got.append(swap(jnp.stack([part[z] for part in both]), "shard", 2 * z))
    return jnp.stack(got, axis=1)


def scatter_sum(parts):
    half = parts.shape[1]
    pair = (parts[0].astype(F32) + swap(parts[1], "shard", 1).astype(F32)).astype(parts.dtype)
    total = pair[0].astype(F32)
    for z in range(1, half):
        total = total + swap(pair[z], "shard", 2 * z).astype(F32)
    return total


def gather_rows(rows):
    half = lax.axis_size("shard") // 2
    column = jnp.stack([rows] + [swap(rows, "shard", 2 * z) for z in range(1, half)])
    return jnp.stack([column, swap(column, "shard", 1)])


def exchange(value):
    count = lax.axis_size("section")
    out = [value]
    for step in range(1, count):
        pairs = [(i, i ^ step) for i in range(1, count) if i ^ step > 0]
        out.append(lax.ppermute(value, "section", pairs))
    return out


def pick(values, distance):
    result = values[0]
    for step in range(1, len(values)):
        result = jnp.where(distance == step, values[step], result)
    return result


def dot_t(left, right):
    return lax.dot_general(left, right, (((1,), (1,)), ((), ())), preferred_element_type=F32)


def per_device(
    activations,
    top_grad,
    loss_mask,
    norm_gain,
    value_weight,
    output_weight,
    value_proj,
    grad_proj,
    store,
):
    sections = lax.axis_size("section")
    section = lax.axis_index("section")
    shards = lax.axis_size("shard")
    shard = lax.axis_index("shard")
    hidden = activations[0]
    tokens, width = hidden.shape
    kv = value_weight.shape[2]
    proj = value_proj.shape[2]
    columns = width // shards
    half = shards // 2
    groups = sections - 1
    rows = -(-tokens // groups)
    rows = -(-rows // 16) * 16
    padded = rows * groups
    block = shards * rows
    group = jnp.maximum(section - 1, 0)

    gain = norm_gain[0]
    gain_slice = lax.dynamic_slice_in_dim(gain, shard * columns, columns, 0)
    value_scaled = (value_weight[0].astype(F32) * gain_slice[:, None]).astype(BF16)

    hidden_padded = jnp.pad(hidden, ((0, padded - tokens), (0, 0)))

    def rows_of(array, which):
        return lax.dynamic_slice_in_dim(array, which * rows, rows, 0)

    hidden_rows = [rows_of(hidden_padded, group)]
    for step in range(1, sections):
        pairs = [(i, i ^ step) for i in range(1, sections) if i ^ step > 0]
        sent = rows_of(hidden_padded, jnp.maximum((section ^ step) - 1, 0))
        hidden_rows.append(lax.ppermute(sent, "section", pairs))

    output_from = exchange(output_weight[0])
    value_from = exchange(value_scaled)
    proj_slice = lax.dynamic_slice_in_dim(grad_proj[0], shard * columns, columns, 0)
    proj_from = [proj_slice] + [swap(proj_slice, "section", step) for step in range(1, sections)]

    cotangent = (top_grad.astype(F32) * loss_mask.astype(F32)[:, None]).astype(BF16)
    cotangent_rows = rows_of(jnp.pad(cotangent, ((0, padded - tokens), (0, 0))), group)
    state = spread(cotangent_rows).reshape(block, columns).astype(F32)

    layer_rows = jnp.concatenate([pick(hidden_rows, layer ^ section) for layer in range(1, sections)])
    layer_f32 = layer_rows.astype(F32).reshape(groups, rows, width)
    inverse_rows = lax.rsqrt(jnp.mean(layer_f32 * layer_f32, axis=-1, keepdims=True) + EPSILON)
    layer_columns = spread(layer_rows)
    layer_columns = layer_columns.reshape(2, half, groups, rows, columns)

    def hidden_of(layer):
        return layer_columns[:, :, layer - 1].reshape(block, columns)

    hidden_f32 = hidden.astype(F32)
    inverse = lax.rsqrt(jnp.mean(hidden_f32 * hidden_f32, axis=-1, keepdims=True) + EPSILON)
    normed = (hidden_f32 * inverse * gain).astype(BF16)
    low_slice = jnp.dot(value_weight[0], value_proj[0], preferred_element_type=F32).astype(BF16)
    low_full = lax.all_gather(low_slice, "shard", axis=0, tiled=True)
    value_low = jnp.dot(normed, low_full, preferred_element_type=F32)
    grad_low_top = jnp.dot(cotangent, grad_proj[0], preferred_element_type=F32)

    def by_shard(value):
        return value.reshape(2, half, rows, value.shape[1])

    low_parts = []
    scalar = None
    for layer in range(sections - 1, 0, -1):
        output_layer = pick(output_from, layer ^ section)
        value_layer = pick(value_from, layer ^ section)
        inverse_layer = inverse_rows[layer - 1]
        sent = [dot_t(state.astype(BF16), output_layer).astype(BF16)]
        if scalar is not None:
            sent.append(dot_t(hidden_of(layer + 1), output_layer).astype(BF16))
            sent.append(jnp.broadcast_to(scalar, (block, 128)).astype(BF16))
        total = scatter_sum(by_shard(jnp.concatenate(sent, axis=1)))
        grad_value = total[:, :kv]
        if scalar is not None:
            inverse_above = inverse_rows[layer]
            factor = total[:, 2 * kv : 2 * kv + 1] * (inverse_above * inverse_above / width)
            grad_value = grad_value - factor * total[:, kv : 2 * kv]
        back = [(grad_value * inverse_layer).astype(BF16)]
        if scalar is not None:
            back.append(jnp.broadcast_to(factor, (rows, 128)).astype(BF16))
        full = gather_rows(jnp.concatenate(back, axis=1)).reshape(block, -1)
        if scalar is not None:
            state = state - full[:, kv : kv + 1].astype(F32) * hidden_of(layer + 1).astype(F32)
            low_parts.append(
                jnp.dot(state.astype(BF16), pick(proj_from, layer ^ section), preferred_element_type=F32)
            )
        change = dot_t(full[:, :kv], value_layer)
        state = state + change
        scalar = jnp.sum(change * hidden_of(layer).astype(F32), axis=1, keepdims=True)
    proj_first = pick(proj_from, section)
    low_parts.append(jnp.dot(state.astype(BF16), proj_first, preferred_element_type=F32))
    low_parts.append(jnp.dot(hidden_of(1), proj_first, preferred_element_type=F32))
    low_parts.append(jnp.broadcast_to(scalar, (block, proj)))
    low = scatter_sum(by_shard(jnp.concatenate(low_parts, axis=1)))
    low = low.reshape(rows, sections + 1, proj)
    inverse_first = inverse_rows[0]
    factor = low[:, sections, :1] * (inverse_first * inverse_first / width)
    low_first = low[:, sections - 2] - factor * low[:, sections - 1]
    low_layers = jnp.stack([low_first] + [low[:, sections - 2 - layer] for layer in range(1, sections - 1)] + [low_first])

    own = lax.dynamic_index_in_dim(low_layers, section, 0, keepdims=False)
    got = [own]
    for step in range(1, sections):
        got.append(
            swap(lax.dynamic_index_in_dim(low_layers, section ^ step, 0, keepdims=False), "section", step)
        )
    got = jnp.stack(got)
    grad_low = jnp.concatenate(
        [lax.dynamic_index_in_dim(got, section ^ source, 0, keepdims=False) for source in range(1, sections)]
    )[:tokens]
    grad_low = jnp.where(section == sections - 1, grad_low_top, grad_low)

    gens = tokens // LEN
    features = jnp.einsum(
        "gta,gtb->gab",
        grad_low.reshape(gens, LEN, proj),
        value_low.reshape(gens, LEN, proj),
        precision=lax.Precision.HIGHEST,
    ).reshape(gens, proj * proj)
    gathered = gather_rows(features)
    gathered = gathered.transpose(1, 0, 2, 3).reshape(shards, gens, proj * proj)
    gathered = jnp.stack(
        [lax.dynamic_index_in_dim(gathered, shard ^ i, 0, keepdims=False) for i in range(shards)]
    ).reshape(shards * gens, proj * proj)
    partial = lax.dot_general(
        gathered,
        store[0],
        (((1,), (1,)), ((), ())),
        precision=lax.Precision.HIGHEST,
        preferred_element_type=F32,
    )
    rows_out = partial.shape[0] // sections
    result = lax.dynamic_slice_in_dim(partial, section * rows_out, rows_out, 0)
    for step in range(1, sections):
        sent = lax.dynamic_slice_in_dim(partial, (section ^ step) * rows_out, rows_out, 0)
        result = result + swap(sent, "section", step)
    return result


def solution(mesh):
    placed = (
        P("section", "shard", None),
        P("shard", None),
        P("shard"),
        P("section", None),
        P("section", "shard", None),
        P("section", None, "shard"),
        P("section", None, None),
        P("section", None, None),
        P("section", "shard", None),
    )
    return jax.shard_map(
        per_device, mesh=mesh, in_specs=placed, out_specs=P("section", "shard"), check_vma=False
    )
```

```python
import jax
import jax.numpy as jnp
from jax import lax
from jax.experimental import pallas as pl
from jax.experimental.pallas import tpu as pltpu
from jax.sharding import PartitionSpec as P

LEN = 96
EPSILON = 1e-05
BF16 = jnp.bfloat16
F32 = jnp.float32


def swap(value, axis, step):
    return lax.ppermute(value, axis, [(i, i ^ step) for i in range(lax.axis_size(axis))])


def radices(count):
    digits = []
    while count > 1:
        digit = 4 if count % 4 == 0 else 2
        digits.append(digit)
        count //= digit
    return digits


def step_list(rest, digit):
    return [2 * rest * place for place in range(1, digit)]


def scatter_terms(parts):
    digits = radices(parts.shape[0])
    for place, digit in enumerate(digits):
        rest = parts.shape[0] // digit
        split = parts.reshape((digit, rest) + parts.shape[1:])
        got = [split[0]] + [swap(split[j + 1], "shard", step) for j, step in enumerate(step_list(rest, digit))]
        if place == len(digits) - 1:
            return [value.reshape(parts.shape[1:]) for value in got]
        parts = sum(value.astype(F32) for value in got).astype(parts.dtype)
    return [parts.reshape(parts.shape[1:])]


def scatter_sum(parts):
    return sum(value.astype(F32) for value in scatter_terms(parts))


def gather_pieces(rows):
    values = [rows]
    chips = lax.axis_size("shard") // 2
    for digit in reversed(radices(chips)):
        value = values[0] if len(values) == 1 else jnp.concatenate(values)
        rest = value.shape[0] // rows.shape[0]
        values = [value] + [swap(value, "shard", step) for step in step_list(rest, digit)]
    return values


def gather_chips(rows):
    return jnp.concatenate(gather_pieces(rows)).reshape((-1,) + rows.shape)


def spread(pieces):
    chips = pieces.shape[0]
    tail = pieces.shape[1:]
    done = 1
    value = pieces.reshape((1, chips) + tail)
    for digit in radices(chips):
        rest = value.shape[1] // digit
        value = value.reshape((done, digit, rest) + tail)
        got = [value[:, 0]]
        for j, step in enumerate(step_list(rest, digit)):
            got.append(swap(value[:, j + 1], "shard", step))
        value = jnp.stack(got, axis=1)
        done = done * digit
        value = value.reshape((done, rest) + tail)
    return value.reshape((chips,) + tail)


def exchange(value, steps, sections):
    return {
        step: lax.ppermute(value, "section", [(i, i ^ step) for i in range(1, sections) if i ^ step > 0])
        for step in steps
    }


def ways(layer, sections):
    return sorted(layer ^ other for other in range(1, sections))


def choose_body(which, *refs):
    *sources, target, sem = refs
    for place, source in enumerate(sources):

        @pl.when(which[0] == place)
        def _():
            copy = pltpu.make_async_copy(source, target, sem)
            copy.start()
            copy.wait()


def choose(values, layer, section, sections):
    keys = ways(layer, sections)
    which = jnp.int32(0)
    for place, key in enumerate(keys):
        which = jnp.where((layer ^ section) == key, place, which)
    value = values[keys[0]]
    return pl.pallas_call(
        choose_body,
        out_shape=jax.ShapeDtypeStruct(value.shape, value.dtype),
        in_specs=[pl.BlockSpec(memory_space=pltpu.SMEM)] + [pl.BlockSpec(memory_space=pl.ANY)] * len(keys),
        out_specs=pl.BlockSpec(memory_space=pltpu.VMEM),
        scratch_shapes=[pltpu.SemaphoreType.DMA],
        cost_estimate=pl.CostEstimate(flops=0, bytes_accessed=2 * value.size * 2, transcendentals=0),
    )(which.reshape(1), *[values[key] for key in keys])


def pick(values, layer, section, sections):
    keys = ways(layer, sections)
    distance = layer ^ section
    result = values[keys[0]]
    for key in keys[1:]:
        result = jnp.where(distance == key, values[key], result)
    return result


def dot_t(left, right):
    return lax.dot_general(left, right, (((1,), (1,)), ((), ())), preferred_element_type=F32)


PARAMS = pltpu.CompilerParams(vmem_limit_bytes=36 * 1024 * 1024)


def rows_body(width, *refs):
    *addends, act, out = refs
    kv = addends[0].shape[1]
    total = addends[0][...].astype(F32)
    for value in addends[1:]:
        total = total + value[...].astype(F32)
    inverse = act[:, kv : kv + 1].astype(F32) + act[:, kv + 64 : kv + 65].astype(F32)
    grad_value = total * inverse
    factor = jnp.sum(grad_value * act[:, :kv].astype(F32), axis=1, keepdims=True) * inverse / width
    out[:, :kv] = grad_value.astype(BF16)
    out[:, kv:] = jnp.broadcast_to(factor, (factor.shape[0], out.shape[1] - kv)).astype(BF16)


def rows_step(addends, act, width):
    rows, kv = addends[0].shape
    return pl.pallas_call(
        lambda *refs: rows_body(width, *refs),
        out_shape=jax.ShapeDtypeStruct(act.shape, BF16),
        compiler_params=PARAMS,
        cost_estimate=pl.CostEstimate(flops=8 * rows * kv, bytes_accessed=16 * rows * kv, transcendentals=0),
    )(*addends, act)


def layer_body(last, *refs):
    *pieces, state, hidden, value_near, value_far, next_near, next_far, new_state, part, full = refs
    kv = value_near.shape[1]
    columns = value_near.shape[0]
    start = 0
    for piece in pieces:
        full[start : start + piece.shape[0]] = piece[...]
        start += piece.shape[0]
    grad = full[:, :kv]
    factor = full[:, kv : kv + 1].astype(F32)
    total = None
    for place, (value, after_value) in enumerate(((value_near, next_near), (value_far, next_far))):
        here = slice(place * columns, (place + 1) * columns)
        change = dot_t(grad, value[...])
        moved = state[:, here] + change - hidden[:, here].astype(F32) * factor
        new_state[:, here] = moved
        term = dot_t(moved.astype(BF16), after_value[...])
        total = term if total is None else total + term
    part[...] = total.astype(part.dtype)


def layer_step(pieces, state, hidden, value_near, value_far, next_near, next_far, part_dtype):
    block, width = state.shape
    kv = value_near.shape[1]
    outs = next_near.shape[0]
    return pl.pallas_call(
        lambda *refs: layer_body(False, *refs),
        out_shape=(
            jax.ShapeDtypeStruct((block, width), F32),
            jax.ShapeDtypeStruct((block, outs), part_dtype),
        ),
        scratch_shapes=[pltpu.VMEM((block, pieces[0].shape[1]), BF16)],
        compiler_params=PARAMS,
        cost_estimate=pl.CostEstimate(
            flops=2 * block * width * (kv + outs),
            bytes_accessed=2 * width * (kv + outs) + 12 * block * width,
            transcendentals=0,
        ),
    )(*pieces, state, hidden, value_near, value_far, next_near, next_far)


def per_device(
    activations,
    top_grad,
    loss_mask,
    norm_gain,
    value_weight,
    output_weight,
    value_proj,
    grad_proj,
    store,
):
    sections = lax.axis_size("section")
    section = lax.axis_index("section")
    shards = lax.axis_size("shard")
    shard = lax.axis_index("shard")
    hidden = activations[0]
    tokens, width = hidden.shape
    kv = value_weight.shape[2]
    proj = value_proj.shape[2]
    columns = width // shards
    chips = shards // 2
    groups = sections - 1
    rows = -(-tokens // groups)
    rows = -(-rows // 16) * 16
    padded = rows * groups
    block = chips * rows
    group = jnp.maximum(section - 1, 0)
    gens = tokens // LEN

    def chip_columns(array, chip):
        first = shard ^ (2 * chip)
        return jnp.concatenate(
            [
                lax.dynamic_slice_in_dim(array, first * columns, columns, 1),
                lax.dynamic_slice_in_dim(array, (first ^ 1) * columns, columns, 1),
            ],
            axis=1,
        )

    near = [step for step in ways(sections - 1, sections) if step]
    far = [step for step in range(1, sections) if step not in near]
    output_from = {0: output_weight[0], **exchange(output_weight[0], near, sections)}

    cotangent = (top_grad.astype(F32) * loss_mask.astype(F32)[:, None]).astype(BF16)
    cotangent_rows = lax.dynamic_slice_in_dim(
        jnp.pad(cotangent, ((0, padded - tokens), (0, 0))), group * rows, rows, 0
    )
    state = spread(jnp.stack([chip_columns(cotangent_rows, chip) for chip in range(chips)]))
    state = state.reshape(block, 2 * columns)

    hidden_columns = spread(jnp.stack([chip_columns(hidden, chip) for chip in range(chips)]))
    gain_slice = lax.dynamic_slice_in_dim(norm_gain[0], shard * columns, columns, 0)
    value_scaled = (value_weight[0].astype(F32) * gain_slice[:, None]).astype(BF16)
    scaled_far = swap(value_scaled, "shard", 1)

    columns_padded = jnp.pad(hidden_columns, ((0, 0), (0, padded - tokens), (0, 0)))

    def to_groups(array, dim):
        def part(other):
            return lax.dynamic_slice_in_dim(array, jnp.maximum(other - 1, 0) * rows, rows, dim)

        out = {0: part(section)}
        for step in range(1, sections):
            pairs = [(i, i ^ step) for i in range(1, sections) if i ^ step > 0]
            out[step] = lax.ppermute(part(section ^ step), "section", pairs)
        return out

    proj_piece = chip_columns(grad_proj[0].T, 0)

    def message(other):
        part = lax.dynamic_slice_in_dim(columns_padded, jnp.maximum(other - 1, 0) * rows, rows, 1)
        return jnp.concatenate([part.reshape(block, 2 * columns), proj_piece])

    message_from = [message(section)]
    for step in range(1, sections):
        pairs = [(i, i ^ step) for i in range(sections) if i ^ step > 0]
        message_from.append(lax.ppermute(message(section ^ step), "section", pairs))

    flat = hidden_columns.reshape(chips * tokens, 2 * columns)
    part = jnp.dot(flat[:, :columns], value_scaled, preferred_element_type=F32)
    part = part + jnp.dot(flat[:, columns:], scaled_far, preferred_element_type=F32)
    value_sum_terms = scatter_terms(part.astype(BF16).reshape(chips, tokens, kv))
    output_from, state = lax.optimization_barrier((output_from, state))
    value_from = {0: value_scaled, **exchange(value_scaled, near, sections)}
    value_sum_terms, value_from = lax.optimization_barrier((value_sum_terms, value_from))
    value_sum = sum(term.astype(F32) for term in value_sum_terms)
    hidden_f32 = hidden.astype(F32)
    inverse = lax.rsqrt(jnp.mean(hidden_f32 * hidden_f32, axis=-1, keepdims=True) + EPSILON)
    value_act = (value_sum * inverse).astype(BF16)
    value_low = jnp.dot(value_act, value_proj[0], preferred_element_type=F32)
    grad_low_top = jnp.dot(cotangent, grad_proj[0], preferred_element_type=F32)
    inverse_high = inverse.astype(BF16)
    inverse_low = (inverse - inverse_high.astype(F32)).astype(BF16)
    value_rows = jnp.concatenate(
        [
            value_act,
            jnp.broadcast_to(inverse_high, (tokens, 64)),
            jnp.broadcast_to(inverse_low, (tokens, 64)),
        ],
        axis=1,
    )

    value_rows, own_output = lax.optimization_barrier((value_rows, output_weight[0]))
    value_rows_from = to_groups(jnp.pad(value_rows, ((0, padded - tokens), (0, 0))), 0)
    far_output = exchange(own_output, far, sections)

    def message_of(layer):
        distance = layer ^ section
        result = message_from[0]
        for step in range(1, sections):
            result = jnp.where(distance == step, message_from[step], result)
        return result

    output_near = choose(output_from, sections - 1, section, sections)
    output_far = swap(output_near, "shard", 1)
    part = dot_t(state[:, :columns], output_near) + dot_t(state[:, columns:], output_far)
    part = part.astype(BF16)
    state = state.astype(F32)
    low_parts = []
    for layer in range(sections - 1, 0, -1):
        terms = scatter_terms(part.reshape(chips, rows, kv))
        if layer == max(sections - 2, 1) and sections > 2:
            terms, mine = lax.optimization_barrier((terms, mine))
        if layer == sections - 1:
            terms, value_rows_from, message_from, own_value = lax.optimization_barrier(
                (terms, value_rows_from, message_from, value_scaled)
            )
            output_from.update(far_output)
            value_from.update(exchange(own_value, far, sections))
            messages = [message_of(place) for place in range(sections)]
        act = pick(value_rows_from, layer, section, sections)
        pieces = gather_pieces(rows_step(terms, act, width))
        value_near = choose(value_from, layer, section, sections)
        value_far = swap(value_near, "shard", 1)
        if layer < sections - 1:
            low_parts.append(dot_t(state.astype(BF16), messages[layer][block:]))
        if layer > 1:
            next_near = choose(output_from, layer - 1, section, sections)
            next_far = swap(next_near, "shard", 1)
        else:
            next_near = messages[0][block:, :columns]
            next_far = messages[0][block:, columns:]
        state, part = layer_step(
            pieces,
            state,
            messages[layer][:block],
            value_near,
            value_far,
            next_near,
            next_far,
            BF16 if layer > 1 else F32,
        )
        if layer == sections - 1:
            mine = gather_chips(jnp.concatenate([value_low, grad_low_top], axis=1))
            mine = jnp.concatenate([mine, swap(mine, "shard", 1)])
    low_parts.append(part)
    low = jnp.concatenate(low_parts, axis=1).astype(BF16)
    low = sum_chips(low.reshape(chips, rows, groups * proj))
    low = jnp.concatenate([low, swap(low, "shard", 1)]).reshape(shards, rows, groups * proj)
    low_layers = jnp.stack(
        [low[:, :, place * proj : (place + 1) * proj] for place in range(groups - 1, -1, -1)] + [low[:, :, :proj]]
    )

    got = [lax.dynamic_index_in_dim(low_layers, section, 0, keepdims=False)]
    for step in range(1, sections):
        got.append(
            swap(
                lax.dynamic_index_in_dim(low_layers, section ^ step, 0, keepdims=False).astype(BF16),
                "section",
                step,
            ).astype(F32)
        )

    def source_rows(source):
        result = got[0]
        for step in range(1, sections):
            result = jnp.where((section ^ source) == step, got[step], result)
        return result

    grad_low = jnp.concatenate([source_rows(source) for source in range(1, sections)], axis=1)[:, :tokens]
    grad_low = jnp.where(section == sections - 1, mine[:, :, proj:], grad_low)

    features = jnp.einsum(
        "gta,gtb->gab",
        grad_low.reshape(shards * gens, LEN, proj),
        mine[:, :, :proj].reshape(shards * gens, LEN, proj),
        precision=lax.Precision.HIGHEST,
    ).reshape(shards * gens, proj * proj)
    partial = lax.dot_general(
        features,
        store[0],
        (((1,), (1,)), ((), ())),
        precision=lax.Precision.HIGHEST,
        preferred_element_type=F32,
    ).reshape(2, chips, gens, -1)

    def of_shard(index):
        away = shard ^ index
        return lax.dynamic_slice(partial, (away % 2, away // 2, 0, 0), (1, 1) + partial.shape[2:])[0, 0]

    partial = jnp.concatenate([of_shard(i) for i in range(shards)])
    rows_out = partial.shape[0] // sections
    result = lax.dynamic_slice_in_dim(partial, section * rows_out, rows_out, 0)
    for step in range(1, sections):
        sent = lax.dynamic_slice_in_dim(partial, (section ^ step) * rows_out, rows_out, 0)
        result = result + swap(sent, "section", step)
    return result


def sum_chips(value):
    chips = value.shape[0]
    rest = 1
    sent_as = value.dtype
    for digit in reversed(radices(chips)):
        steps = step_list(rest, digit)
        got = [swap(value.astype(sent_as), "shard", step) for step in steps]
        value = value.astype(F32)
        for step, other in zip(steps, got):
            value = value + jnp.stack([other[chip ^ (step // 2)] for chip in range(chips)]).astype(F32)
        rest = rest * digit
    return value


def solution(mesh):
    placed = (
        P("section", "shard", None),
        P("shard", None),
        P("shard"),
        P("section", None),
        P("section", "shard", None),
        P("section", None, "shard"),
        P("section", None, None),
        P("section", None, None),
        P("section", "shard", None),
    )
    return jax.shard_map(
        per_device, mesh=mesh, in_specs=placed, out_specs=P("section", "shard"), check_vma=False
    )
```

```python
import jax
import jax.numpy as jnp
from jax import lax
from jax.experimental import pallas as pl
from jax.experimental.pallas import tpu as pltpu
from jax.sharding import PartitionSpec as P

LEN = 96
EPSILON = 1e-05
BF16 = jnp.bfloat16
F32 = jnp.float32


def swap(value, axis, step):
    return lax.ppermute(value, axis, [(i, i ^ step) for i in range(lax.axis_size(axis))])


def radices(count):
    digits = []
    while count > 1:
        digit = 4 if count % 4 == 0 else 2
        digits.append(digit)
        count //= digit
    return digits


def step_list(rest, digit):
    return [2 * rest * place for place in range(1, digit)]


def scatter_terms(parts):
    digits = radices(parts.shape[0])
    for place, digit in enumerate(digits):
        rest = parts.shape[0] // digit
        split = parts.reshape((digit, rest) + parts.shape[1:])
        got = [split[0]] + [swap(split[j + 1], "shard", step) for j, step in enumerate(step_list(rest, digit))]
        if place == len(digits) - 1:
            return [value.reshape(parts.shape[1:]) for value in got]
        parts = sum(value.astype(F32) for value in got).astype(parts.dtype)
    return [parts.reshape(parts.shape[1:])]


def scatter_sum(parts):
    return sum(value.astype(F32) for value in scatter_terms(parts))


def gather_pieces(rows):
    values = [rows]
    chips = lax.axis_size("shard") // 2
    for digit in reversed(radices(chips)):
        value = values[0] if len(values) == 1 else jnp.concatenate(values)
        rest = value.shape[0] // rows.shape[0]
        values = [value] + [swap(value, "shard", step) for step in step_list(rest, digit)]
    return values


def gather_chips(rows):
    return jnp.concatenate(gather_pieces(rows)).reshape((-1,) + rows.shape)


def spread(pieces):
    chips = pieces.shape[0]
    tail = pieces.shape[1:]
    done = 1
    value = pieces.reshape((1, chips) + tail)
    for digit in radices(chips):
        rest = value.shape[1] // digit
        value = value.reshape((done, digit, rest) + tail)
        got = [value[:, 0]]
        for j, step in enumerate(step_list(rest, digit)):
            got.append(swap(value[:, j + 1], "shard", step))
        value = jnp.stack(got, axis=1)
        done = done * digit
        value = value.reshape((done, rest) + tail)
    return value.reshape((chips,) + tail)


def exchange(value, steps, sections):
    return {
        step: lax.ppermute(value, "section", [(i, i ^ step) for i in range(1, sections) if i ^ step > 0])
        for step in steps
    }


def ways(layer, sections):
    return sorted(layer ^ other for other in range(1, sections))


def choose_body(which, *refs):
    *sources, target, sem = refs
    for place, source in enumerate(sources):

        @pl.when(which[0] == place)
        def _():
            copy = pltpu.make_async_copy(source, target, sem)
            copy.start()
            copy.wait()


def choose(values, layer, section, sections):
    keys = ways(layer, sections)
    which = jnp.int32(0)
    for place, key in enumerate(keys):
        which = jnp.where((layer ^ section) == key, place, which)
    value = values[keys[0]]
    return pl.pallas_call(
        choose_body,
        out_shape=jax.ShapeDtypeStruct(value.shape, value.dtype),
        in_specs=[pl.BlockSpec(memory_space=pltpu.SMEM)] + [pl.BlockSpec(memory_space=pl.ANY)] * len(keys),
        out_specs=pl.BlockSpec(memory_space=pltpu.VMEM),
        scratch_shapes=[pltpu.SemaphoreType.DMA],
        cost_estimate=pl.CostEstimate(flops=0, bytes_accessed=2 * value.size * 2, transcendentals=0),
    )(which.reshape(1), *[values[key] for key in keys])


def pick(values, layer, section, sections):
    keys = ways(layer, sections)
    distance = layer ^ section
    result = values[keys[0]]
    for key in keys[1:]:
        result = jnp.where(distance == key, values[key], result)
    return result


def dot_t(left, right):
    return lax.dot_general(left, right, (((1,), (1,)), ((), ())), preferred_element_type=F32)


PARAMS = pltpu.CompilerParams(vmem_limit_bytes=36 * 1024 * 1024)


def rows_body(width, *refs):
    *addends, act, out = refs
    kv = addends[0].shape[1]
    total = addends[0][...].astype(F32)
    for value in addends[1:]:
        total = total + value[...].astype(F32)
    inverse = act[:, kv : kv + 1].astype(F32) + act[:, kv + 64 : kv + 65].astype(F32)
    grad_value = total * inverse
    factor = jnp.sum(grad_value * act[:, :kv].astype(F32), axis=1, keepdims=True) * inverse / width
    out[:, :kv] = grad_value.astype(BF16)
    out[:, kv:] = jnp.broadcast_to(factor, (factor.shape[0], out.shape[1] - kv)).astype(BF16)


def rows_step(addends, act, width):
    rows, kv = addends[0].shape
    return pl.pallas_call(
        lambda *refs: rows_body(width, *refs),
        out_shape=jax.ShapeDtypeStruct(act.shape, BF16),
        compiler_params=PARAMS,
        cost_estimate=pl.CostEstimate(flops=8 * rows * kv, bytes_accessed=16 * rows * kv, transcendentals=0),
    )(*addends, act)


def layer_body(last, *refs):
    *pieces, state, hidden, value_near, value_far, next_near, next_far, new_state, part, full = refs
    kv = value_near.shape[1]
    columns = value_near.shape[0]
    start = 0
    for piece in pieces:
        full[start : start + piece.shape[0]] = piece[...]
        start += piece.shape[0]
    grad = full[:, :kv]
    factor = full[:, kv : kv + 1].astype(F32)
    total = None
    for place, (value, after_value) in enumerate(((value_near, next_near), (value_far, next_far))):
        here = slice(place * columns, (place + 1) * columns)
        change = dot_t(grad, value[...])
        moved = state[:, here] + change - hidden[:, here].astype(F32) * factor
        new_state[:, here] = moved
        term = dot_t(moved.astype(BF16), after_value[...])
        total = term if total is None else total + term
    part[...] = total.astype(part.dtype)


def layer_step(pieces, state, hidden, value_near, value_far, next_near, next_far, part_dtype):
    block, width = state.shape
    kv = value_near.shape[1]
    outs = next_near.shape[0]
    return pl.pallas_call(
        lambda *refs: layer_body(False, *refs),
        out_shape=(
            jax.ShapeDtypeStruct((block, width), F32),
            jax.ShapeDtypeStruct((block, outs), part_dtype),
        ),
        scratch_shapes=[pltpu.VMEM((block, pieces[0].shape[1]), BF16)],
        compiler_params=PARAMS,
        cost_estimate=pl.CostEstimate(
            flops=2 * block * width * (kv + outs),
            bytes_accessed=2 * width * (kv + outs) + 12 * block * width,
            transcendentals=0,
        ),
    )(*pieces, state, hidden, value_near, value_far, next_near, next_far)


def per_device(
    activations,
    top_grad,
    loss_mask,
    norm_gain,
    value_weight,
    output_weight,
    value_proj,
    grad_proj,
    store,
):
    sections = lax.axis_size("section")
    section = lax.axis_index("section")
    shards = lax.axis_size("shard")
    shard = lax.axis_index("shard")
    hidden = activations[0]
    tokens, width = hidden.shape
    kv = value_weight.shape[2]
    proj = value_proj.shape[2]
    columns = width // shards
    chips = shards // 2
    groups = sections - 1
    rows = -(-tokens // groups)
    rows = -(-rows // 16) * 16
    padded = rows * groups
    block = chips * rows
    group = jnp.maximum(section - 1, 0)
    gens = tokens // LEN

    def chip_columns(array, chip):
        first = shard ^ (2 * chip)
        return jnp.concatenate(
            [
                lax.dynamic_slice_in_dim(array, first * columns, columns, 1),
                lax.dynamic_slice_in_dim(array, (first ^ 1) * columns, columns, 1),
            ],
            axis=1,
        )

    near = [step for step in ways(sections - 1, sections) if step]
    far = [step for step in range(1, sections) if step not in near]
    output_from = {0: output_weight[0], **exchange(output_weight[0], near, sections)}

    cotangent = (top_grad.astype(F32) * loss_mask.astype(F32)[:, None]).astype(BF16)
    cotangent_rows = lax.dynamic_slice_in_dim(
        jnp.pad(cotangent, ((0, padded - tokens), (0, 0))), group * rows, rows, 0
    )
    state = spread(jnp.stack([chip_columns(cotangent_rows, chip) for chip in range(chips)]))
    state = state.reshape(block, 2 * columns)

    hidden_columns = spread(jnp.stack([chip_columns(hidden, chip) for chip in range(chips)]))
    gain_slice = lax.dynamic_slice_in_dim(norm_gain[0], shard * columns, columns, 0)
    value_scaled = (value_weight[0].astype(F32) * gain_slice[:, None]).astype(BF16)
    scaled_far = swap(value_scaled, "shard", 1)

    columns_padded = jnp.pad(hidden_columns, ((0, 0), (0, padded - tokens), (0, 0)))

    def to_groups(array, dim):
        def part(other):
            return lax.dynamic_slice_in_dim(array, jnp.maximum(other - 1, 0) * rows, rows, dim)

        out = {0: part(section)}
        for step in range(1, sections):
            pairs = [(i, i ^ step) for i in range(1, sections) if i ^ step > 0]
            out[step] = lax.ppermute(part(section ^ step), "section", pairs)
        return out

    columns_from = to_groups(columns_padded, 1)
    proj_piece = chip_columns(grad_proj[0].T, 0)

    flat = hidden_columns.reshape(chips * tokens, 2 * columns)
    part = jnp.dot(flat[:, :columns], value_scaled, preferred_element_type=F32)
    part = part + jnp.dot(flat[:, columns:], scaled_far, preferred_element_type=F32)
    value_sum_terms = scatter_terms(part.astype(BF16).reshape(chips, tokens, kv))
    output_from, state = lax.optimization_barrier((output_from, state))
    value_from = {0: value_scaled, **exchange(value_scaled, near, sections)}
    value_sum_terms, value_from = lax.optimization_barrier((value_sum_terms, value_from))
    value_sum = sum(term.astype(F32) for term in value_sum_terms)
    hidden_f32 = hidden.astype(F32)
    inverse = lax.rsqrt(jnp.mean(hidden_f32 * hidden_f32, axis=-1, keepdims=True) + EPSILON)
    value_act = (value_sum * inverse).astype(BF16)
    value_low = jnp.dot(value_act, value_proj[0], preferred_element_type=F32)
    grad_low_top = jnp.dot(cotangent, grad_proj[0], preferred_element_type=F32)
    inverse_high = inverse.astype(BF16)
    inverse_low = (inverse - inverse_high.astype(F32)).astype(BF16)
    value_rows = jnp.concatenate(
        [
            value_act,
            jnp.broadcast_to(inverse_high, (tokens, 64)),
            jnp.broadcast_to(inverse_low, (tokens, 64)),
        ],
        axis=1,
    )

    value_rows, own_output, columns_from = lax.optimization_barrier((value_rows, output_weight[0], columns_from))
    value_rows_from = to_groups(jnp.pad(value_rows, ((0, padded - tokens), (0, 0))), 0)
    far_output = exchange(own_output, far, sections)

    output_near = choose(output_from, sections - 1, section, sections)
    output_far = swap(output_near, "shard", 1)
    part = dot_t(state[:, :columns], output_near) + dot_t(state[:, columns:], output_far)
    part = part.astype(BF16)
    state = state.astype(F32)
    low_parts = []
    for layer in range(sections - 1, 0, -1):
        terms = scatter_terms(part.reshape(chips, rows, kv))
        if layer == max(sections - 2, 1) and sections > 2:
            terms, mine = lax.optimization_barrier((terms, mine))
        if layer == sections - 1:
            terms, value_rows_from, own_value = lax.optimization_barrier((terms, value_rows_from, value_scaled))
            value_from.update(exchange(own_value, far, sections))

        def proj_of(place):
            result = proj_from[0]
            for step in range(1, sections):
                result = jnp.where((place ^ section) == step, proj_from[step], result)
            return result

        act = pick(value_rows_from, layer, section, sections)
        pieces = gather_pieces(rows_step(terms, act, width))
        if layer == sections - 1:
            pieces, far_output = lax.optimization_barrier((pieces, far_output))
            output_from.update(far_output)
        value_near = choose(value_from, layer, section, sections)
        value_far = swap(value_near, "shard", 1)
        if layer < sections - 1:
            low_parts.append(dot_t(state.astype(BF16), proj_of(layer)))
        if layer > 1:
            next_near = choose(output_from, layer - 1, section, sections)
            next_far = swap(next_near, "shard", 1)
        else:
            first = proj_of(0)
            next_near = first[:, :columns]
            next_far = first[:, columns:]
        state, part = layer_step(
            pieces,
            state,
            pick(columns_from, layer, section, sections).reshape(block, 2 * columns),
            value_near,
            value_far,
            next_near,
            next_far,
            BF16 if layer > 1 else F32,
        )
        if layer == sections - 1:
            mine = jnp.concatenate([value_low, grad_low_top], axis=1)
            state, part, mine, proj_piece, value_from, output_from = lax.optimization_barrier(
                (state, part, mine, proj_piece, value_from, output_from)
            )
            proj_from = [proj_piece]
            for step in range(1, sections):
                pairs = [(i, i ^ step) for i in range(sections - 1) if i ^ step > 0]
                proj_from.append(lax.ppermute(proj_piece, "section", pairs))
            mine = gather_chips(mine)
            mine = jnp.concatenate([mine, swap(mine, "shard", 1)])
    low_parts.append(part)
    low = jnp.concatenate(low_parts, axis=1).astype(BF16)
    low = sum_chips(low.reshape(chips, rows, groups * proj))
    low = jnp.concatenate([low, swap(low, "shard", 1)]).reshape(shards, rows, groups * proj)
    low_layers = jnp.stack(
        [low[:, :, place * proj : (place + 1) * proj] for place in range(groups - 1, -1, -1)] + [low[:, :, :proj]]
    )

    got = [lax.dynamic_index_in_dim(low_layers, section, 0, keepdims=False)]
    for step in range(1, sections):
        got.append(
            swap(
                lax.dynamic_index_in_dim(low_layers, section ^ step, 0, keepdims=False).astype(BF16),
                "section",
                step,
            ).astype(F32)
        )

    def source_rows(source):
        result = got[0]
        for step in range(1, sections):
            result = jnp.where((section ^ source) == step, got[step], result)
        return result

    grad_low = jnp.concatenate([source_rows(source) for source in range(1, sections)], axis=1)[:, :tokens]
    grad_low = jnp.where(section == sections - 1, mine[:, :, proj:], grad_low)

    features = jnp.einsum(
        "gta,gtb->gab",
        grad_low.reshape(shards * gens, LEN, proj),
        mine[:, :, :proj].reshape(shards * gens, LEN, proj),
        precision=lax.Precision.HIGHEST,
    ).reshape(shards * gens, proj * proj)
    partial = lax.dot_general(
        features,
        store[0],
        (((1,), (1,)), ((), ())),
        precision=lax.Precision.HIGHEST,
        preferred_element_type=F32,
    ).reshape(2, chips, gens, -1)

    def of_shard(index):
        away = shard ^ index
        return lax.dynamic_slice(partial, (away % 2, away // 2, 0, 0), (1, 1) + partial.shape[2:])[0, 0]

    partial = jnp.concatenate([of_shard(i) for i in range(shards)])
    rows_out = partial.shape[0] // sections
    result = lax.dynamic_slice_in_dim(partial, section * rows_out, rows_out, 0)
    for step in range(1, sections):
        sent = lax.dynamic_slice_in_dim(partial, (section ^ step) * rows_out, rows_out, 0)
        result = result + swap(sent, "section", step)
    return result


def sum_chips(value):
    chips = value.shape[0]
    rest = 1
    sent_as = value.dtype
    for digit in reversed(radices(chips)):
        steps = step_list(rest, digit)
        got = [swap(value.astype(sent_as), "shard", step) for step in steps]
        value = value.astype(F32)
        for step, other in zip(steps, got):
            value = value + jnp.stack([other[chip ^ (step // 2)] for chip in range(chips)]).astype(F32)
        rest = rest * digit
    return value


def solution(mesh):
    placed = (
        P("section", "shard", None),
        P("shard", None),
        P("shard"),
        P("section", None),
        P("section", "shard", None),
        P("section", None, "shard"),
        P("section", None, None),
        P("section", None, None),
        P("section", "shard", None),
    )
    return jax.shard_map(
        per_device, mesh=mesh, in_specs=placed, out_specs=P("section", "shard"), check_vma=False
    )
```

```python
import jax
import jax.numpy as jnp
from jax import lax
from jax.experimental import pallas as pl
from jax.experimental.pallas import tpu as pltpu
from jax.sharding import PartitionSpec as P

LEN = 96
EPSILON = 1e-05
BF16 = jnp.bfloat16
F32 = jnp.float32


def swap(value, axis, step):
    return lax.ppermute(value, axis, [(i, i ^ step) for i in range(lax.axis_size(axis))])


def radices(count):
    digits = []
    while count > 1:
        digit = 4 if count % 4 == 0 else 2
        digits.append(digit)
        count //= digit
    return digits


def step_list(rest, digit):
    return [2 * rest * place for place in range(1, digit)]


def scatter_terms(parts):
    digits = radices(parts.shape[0])
    for place, digit in enumerate(digits):
        rest = parts.shape[0] // digit
        split = parts.reshape((digit, rest) + parts.shape[1:])
        got = [split[0]] + [swap(split[j + 1], "shard", step) for j, step in enumerate(step_list(rest, digit))]
        if place == len(digits) - 1:
            return [value.reshape(parts.shape[1:]) for value in got]
        parts = sum(value.astype(F32) for value in got).astype(parts.dtype)
    return [parts.reshape(parts.shape[1:])]


def scatter_sum(parts):
    return sum(value.astype(F32) for value in scatter_terms(parts))


def gather_pieces(rows):
    values = [rows]
    chips = lax.axis_size("shard") // 2
    for digit in reversed(radices(chips)):
        value = values[0] if len(values) == 1 else jnp.concatenate(values)
        rest = value.shape[0] // rows.shape[0]
        values = [value] + [swap(value, "shard", step) for step in step_list(rest, digit)]
    return values


def gather_chips(rows):
    return jnp.concatenate(gather_pieces(rows)).reshape((-1,) + rows.shape)


def spread(pieces):
    chips = pieces.shape[0]
    tail = pieces.shape[1:]
    done = 1
    value = pieces.reshape((1, chips) + tail)
    for digit in radices(chips):
        rest = value.shape[1] // digit
        value = value.reshape((done, digit, rest) + tail)
        got = [value[:, 0]]
        for j, step in enumerate(step_list(rest, digit)):
            got.append(swap(value[:, j + 1], "shard", step))
        value = jnp.stack(got, axis=1)
        done = done * digit
        value = value.reshape((done, rest) + tail)
    return value.reshape((chips,) + tail)


def exchange(value, steps, sections):
    return {
        step: lax.ppermute(value, "section", [(i, i ^ step) for i in range(1, sections) if i ^ step > 0])
        for step in steps
    }


def ways(layer, sections):
    return sorted(layer ^ other for other in range(1, sections))


def choose_body(which, *refs):
    *sources, target, sems = refs
    rows = target.shape[0] // 4
    for place, source in enumerate(sources):

        @pl.when(which[0] == place)
        def _():
            copies = [
                pltpu.make_async_copy(
                    source.at[pl.ds(k * rows, rows)], target.at[pl.ds(k * rows, rows)], sems.at[k]
                )
                for k in range(4)
            ]
            for copy in copies:
                copy.start()
            for copy in copies:
                copy.wait()


def choose(values, layer, section, sections):
    keys = ways(layer, sections)
    which = jnp.int32(0)
    for place, key in enumerate(keys):
        which = jnp.where((layer ^ section) == key, place, which)
    value = values[keys[0]]
    return pl.pallas_call(
        choose_body,
        out_shape=jax.ShapeDtypeStruct(value.shape, value.dtype),
        in_specs=[pl.BlockSpec(memory_space=pltpu.SMEM)] + [pl.BlockSpec(memory_space=pl.ANY)] * len(keys),
        out_specs=pl.BlockSpec(memory_space=pltpu.VMEM),
        scratch_shapes=[pltpu.SemaphoreType.DMA((4,))],
        cost_estimate=pl.CostEstimate(flops=0, bytes_accessed=2 * value.size * 2, transcendentals=0),
    )(which.reshape(1), *[values[key] for key in keys])


def pick(values, layer, section, sections):
    keys = ways(layer, sections)
    distance = layer ^ section
    result = values[keys[0]]
    for key in keys[1:]:
        result = jnp.where(distance == key, values[key], result)
    return result


def dot_t(left, right):
    return lax.dot_general(left, right, (((1,), (1,)), ((), ())), preferred_element_type=F32)


PARAMS = pltpu.CompilerParams(vmem_limit_bytes=36 * 1024 * 1024)


def rows_body(width, *refs):
    *addends, act, out = refs
    kv = addends[0].shape[1]
    total = addends[0][...].astype(F32)
    for value in addends[1:]:
        total = total + value[...].astype(F32)
    inverse = act[:, kv : kv + 1].astype(F32) + act[:, kv + 64 : kv + 65].astype(F32)
    grad_value = total * inverse
    factor = jnp.sum(grad_value * act[:, :kv].astype(F32), axis=1, keepdims=True) * inverse / width
    out[:, :kv] = grad_value.astype(BF16)
    out[:, kv:] = jnp.broadcast_to(factor, (factor.shape[0], out.shape[1] - kv)).astype(BF16)


def rows_step(addends, act, width):
    rows, kv = addends[0].shape
    return pl.pallas_call(
        lambda *refs: rows_body(width, *refs),
        out_shape=jax.ShapeDtypeStruct(act.shape, BF16),
        compiler_params=PARAMS,
        cost_estimate=pl.CostEstimate(flops=8 * rows * kv, bytes_accessed=16 * rows * kv, transcendentals=0),
    )(*addends, act)


def layer_body(last, *refs):
    *pieces, state, hidden, value_near, value_far, next_near, next_far, new_state, part, full = refs
    kv = value_near.shape[1]
    columns = value_near.shape[0]
    start = 0
    for piece in pieces:
        full[start : start + piece.shape[0]] = piece[...]
        start += piece.shape[0]
    grad = full[:, :kv]
    factor = full[:, kv : kv + 1].astype(F32)
    total = None
    for place, (value, after_value) in enumerate(((value_near, next_near), (value_far, next_far))):
        here = slice(place * columns, (place + 1) * columns)
        change = dot_t(grad, value[...])
        moved = state[:, here] + change - hidden[:, here].astype(F32) * factor
        new_state[:, here] = moved
        term = dot_t(moved.astype(BF16), after_value[...])
        total = term if total is None else total + term
    part[...] = total.astype(part.dtype)


def value_step(terms, hidden):
    rows, kv = terms[0].shape
    width = hidden.shape[1]

    def body(*refs):
        *parts, rows_in, out = refs
        wide = rows_in[...].astype(F32)
        inverse = lax.rsqrt(jnp.sum(wide * wide, axis=1, keepdims=True) / width + EPSILON)
        total = parts[0][...].astype(F32)
        for part in parts[1:]:
            total = total + part[...].astype(F32)
        out[:, :kv] = (total * inverse).astype(BF16)
        high = inverse.astype(BF16).astype(F32)
        lane = lax.broadcasted_iota(jnp.int32, (rows, 128), 1)
        out[:, kv:] = jnp.where(lane < 64, high, inverse - high).astype(BF16)

    return pl.pallas_call(
        body,
        out_shape=jax.ShapeDtypeStruct((rows, kv + 128), BF16),
        compiler_params=PARAMS,
        cost_estimate=pl.CostEstimate(
            flops=4 * rows * width, bytes_accessed=2 * rows * (width + 5 * kv), transcendentals=rows
        ),
    )(*terms, hidden)


def layer_step(pieces, state, hidden, value_near, value_far, next_near, next_far, part_dtype):
    block, width = state.shape
    kv = value_near.shape[1]
    outs = next_near.shape[0]
    return pl.pallas_call(
        lambda *refs: layer_body(False, *refs),
        out_shape=(
            jax.ShapeDtypeStruct((block, width), F32),
            jax.ShapeDtypeStruct((block, outs), part_dtype),
        ),
        scratch_shapes=[pltpu.VMEM((block, pieces[0].shape[1]), BF16)],
        compiler_params=PARAMS,
        cost_estimate=pl.CostEstimate(
            flops=2 * block * width * (kv + outs),
            bytes_accessed=2 * width * (kv + outs) + 12 * block * width,
            transcendentals=0,
        ),
    )(*pieces, state, hidden, value_near, value_far, next_near, next_far)


def per_device(
    activations,
    top_grad,
    loss_mask,
    norm_gain,
    value_weight,
    output_weight,
    value_proj,
    grad_proj,
    store,
):
    sections = lax.axis_size("section")
    section = lax.axis_index("section")
    shards = lax.axis_size("shard")
    shard = lax.axis_index("shard")
    hidden = activations[0]
    tokens, width = hidden.shape
    kv = value_weight.shape[2]
    proj = value_proj.shape[2]
    columns = width // shards
    chips = shards // 2
    groups = sections - 1
    rows = -(-tokens // groups)
    rows = -(-rows // 16) * 16
    padded = rows * groups
    block = chips * rows
    group = jnp.maximum(section - 1, 0)
    gens = tokens // LEN

    def chip_columns(array, chip):
        first = shard ^ (2 * chip)
        return jnp.concatenate(
            [
                lax.dynamic_slice_in_dim(array, first * columns, columns, 1),
                lax.dynamic_slice_in_dim(array, (first ^ 1) * columns, columns, 1),
            ],
            axis=1,
        )

    near = [step for step in ways(sections - 1, sections) if step]
    far = [step for step in range(1, sections) if step not in near]
    output_from = {0: output_weight[0], **exchange(output_weight[0], near, sections)}

    cotangent = (top_grad.astype(F32) * loss_mask.astype(F32)[:, None]).astype(BF16)
    cotangent_rows = lax.dynamic_slice_in_dim(
        jnp.pad(cotangent, ((0, padded - tokens), (0, 0))), group * rows, rows, 0
    )
    state = spread(jnp.stack([chip_columns(cotangent_rows, chip) for chip in range(chips)]))
    state = state.reshape(block, 2 * columns)

    hidden_columns = spread(jnp.stack([chip_columns(hidden, chip) for chip in range(chips)]))
    gain_slice = lax.dynamic_slice_in_dim(norm_gain[0], shard * columns, columns, 0)
    value_scaled = (value_weight[0].astype(F32) * gain_slice[:, None]).astype(BF16)
    scaled_far = swap(value_scaled, "shard", 1)

    columns_padded = jnp.pad(hidden_columns, ((0, 0), (0, padded - tokens), (0, 0)))

    def to_groups(array, dim):
        def part(other):
            return lax.dynamic_slice_in_dim(array, jnp.maximum(other - 1, 0) * rows, rows, dim)

        out = {0: part(section)}
        for step in range(1, sections):
            pairs = [(i, i ^ step) for i in range(1, sections) if i ^ step > 0]
            out[step] = lax.ppermute(part(section ^ step), "section", pairs)
        return out

    proj_piece = chip_columns(grad_proj[0].T, 0)

    def message(other):
        part = lax.dynamic_slice_in_dim(columns_padded, jnp.maximum(other - 1, 0) * rows, rows, 1)
        return jnp.concatenate([part.reshape(block, 2 * columns), proj_piece])

    message_from = [message(section)]
    for step in range(1, sections):
        pairs = [(i, i ^ step) for i in range(sections) if i ^ step > 0]
        message_from.append(lax.ppermute(message(section ^ step), "section", pairs))

    flat = hidden_columns.reshape(chips * tokens, 2 * columns)
    part = jnp.dot(flat[:, :columns], value_scaled, preferred_element_type=F32)
    part = part + jnp.dot(flat[:, columns:], scaled_far, preferred_element_type=F32)
    value_sum_terms = scatter_terms(part.astype(BF16).reshape(chips, tokens, kv))
    output_from, state = lax.optimization_barrier((output_from, state))
    value_from = {0: value_scaled, **exchange(value_scaled, near, sections)}
    value_sum_terms, value_from = lax.optimization_barrier((value_sum_terms, value_from))
    value_rows = value_step(value_sum_terms, hidden)
    value_low = jnp.dot(value_rows[:, :kv], value_proj[0], preferred_element_type=F32)
    grad_low_top = jnp.dot(cotangent, grad_proj[0], preferred_element_type=F32)

    value_rows, own_output = lax.optimization_barrier((value_rows, output_weight[0]))
    value_rows_from = to_groups(jnp.pad(value_rows, ((0, padded - tokens), (0, 0))), 0)
    far_output = exchange(own_output, far, sections)

    def message_of(layer):
        distance = layer ^ section
        result = message_from[0]
        for step in range(1, sections):
            result = jnp.where(distance == step, message_from[step], result)
        return result

    output_near = choose(output_from, sections - 1, section, sections)
    output_far = swap(output_near, "shard", 1)
    part = dot_t(state[:, :columns], output_near) + dot_t(state[:, columns:], output_far)
    part = part.astype(BF16)
    state = state.astype(F32)
    low_parts = []
    for layer in range(sections - 1, 0, -1):
        terms = scatter_terms(part.reshape(chips, rows, kv))
        if layer == max(sections - 2, 1) and sections > 2:
            terms, mine = lax.optimization_barrier((terms, mine))
        if layer == sections - 1:
            terms, value_rows_from, message_from, own_value = lax.optimization_barrier(
                (terms, value_rows_from, message_from, value_scaled)
            )
            output_from.update(far_output)
            value_from.update(exchange(own_value, far, sections))
            messages = [message_of(place) for place in range(sections)]
        act = pick(value_rows_from, layer, section, sections)
        pieces = gather_pieces(rows_step(terms, act, width))
        value_near = choose(value_from, layer, section, sections)
        value_far = swap(value_near, "shard", 1)
        if layer < sections - 1:
            low_parts.append(dot_t(state.astype(BF16), messages[layer][block:]))
        if layer > 1:
            next_near = choose(output_from, layer - 1, section, sections)
            next_far = swap(next_near, "shard", 1)
        else:
            next_near = messages[0][block:, :columns]
            next_far = messages[0][block:, columns:]
        state, part = layer_step(
            pieces,
            state,
            messages[layer][:block],
            value_near,
            value_far,
            next_near,
            next_far,
            BF16 if layer > 1 else F32,
        )
        if layer == sections - 1:
            mine = gather_chips(jnp.concatenate([value_low, grad_low_top], axis=1))
            mine = jnp.concatenate([mine, swap(mine, "shard", 1)])
    low_parts.append(part)
    low = jnp.concatenate(low_parts, axis=1).astype(BF16)
    low = sum_chips(low.reshape(chips, rows, groups * proj))
    low = jnp.concatenate([low, swap(low, "shard", 1)]).reshape(shards, rows, groups * proj)
    low_layers = jnp.stack(
        [low[:, :, place * proj : (place + 1) * proj] for place in range(groups - 1, -1, -1)] + [low[:, :, :proj]]
    )

    got = [lax.dynamic_index_in_dim(low_layers, section, 0, keepdims=False)]
    for step in range(1, sections):
        got.append(
            swap(
                lax.dynamic_index_in_dim(low_layers, section ^ step, 0, keepdims=False).astype(BF16),
                "section",
                step,
            ).astype(F32)
        )

    def source_rows(source):
        result = got[0]
        for step in range(1, sections):
            result = jnp.where((section ^ source) == step, got[step], result)
        return result

    grad_low = jnp.concatenate([source_rows(source) for source in range(1, sections)], axis=1)[:, :tokens]
    grad_low = jnp.where(section == sections - 1, mine[:, :, proj:], grad_low)

    features = jnp.einsum(
        "gta,gtb->gab",
        grad_low.reshape(shards * gens, LEN, proj),
        mine[:, :, :proj].reshape(shards * gens, LEN, proj),
        precision=lax.Precision.HIGHEST,
    ).reshape(shards * gens, proj * proj)
    partial = lax.dot_general(
        features,
        store[0],
        (((1,), (1,)), ((), ())),
        precision=lax.Precision.HIGHEST,
        preferred_element_type=F32,
    ).reshape(2, chips, gens, -1)

    def of_shard(index):
        away = shard ^ index
        return lax.dynamic_slice(partial, (away % 2, away // 2, 0, 0), (1, 1) + partial.shape[2:])[0, 0]

    partial = jnp.concatenate([of_shard(i) for i in range(shards)])
    rows_out = partial.shape[0] // sections
    result = lax.dynamic_slice_in_dim(partial, section * rows_out, rows_out, 0)
    for step in range(1, sections):
        sent = lax.dynamic_slice_in_dim(partial, (section ^ step) * rows_out, rows_out, 0)
        result = result + swap(sent, "section", step)
    return result


def sum_chips(value):
    chips = value.shape[0]
    rest = 1
    sent_as = value.dtype
    for digit in reversed(radices(chips)):
        steps = step_list(rest, digit)
        got = [swap(value.astype(sent_as), "shard", step) for step in steps]
        value = value.astype(F32)
        for step, other in zip(steps, got):
            value = value + jnp.stack([other[chip ^ (step // 2)] for chip in range(chips)]).astype(F32)
        rest = rest * digit
    return value


def solution(mesh):
    placed = (
        P("section", "shard", None),
        P("shard", None),
        P("shard"),
        P("section", None),
        P("section", "shard", None),
        P("section", None, "shard"),
        P("section", None, None),
        P("section", None, None),
        P("section", "shard", None),
    )
    return jax.shard_map(
        per_device, mesh=mesh, in_specs=placed, out_specs=P("section", "shard"), check_vma=False
    )
```
